32 devices in a mesh: depth: 2 (over x), row: 4 (over z), col: 4 (over y, core).
Axes of the slice: x: 2, y: 2, z: 4, core: 2. Of those that a mesh axis runs over, the one named last changes fastest.
Arguments:
- inputs: bfloat16 [512, 6144], P('depth', 'row'), may hold values from -6 to 6
- weight: bfloat16 [6144, 24576], P('row', 'col'), may hold values from -0.078125 to 0.078125
- cotangent: bfloat16 [512, 4, 6144], P('depth', 'col', 'row'), may hold values from -6 to 6
Outputs:
- activated: bfloat16 [512, 4, 6144], P('depth', 'col', 'row')
- input_grad: bfloat16 [512, 6144], P('depth', 'row')
- weight_grad: bfloat16 [6144, 4, 6144], P('row', 'col', 'depth')
The draws below stay inside these ranges and needn't reach their ends.
All inputs are finite; a program needn't handle non-finite values.
Results may differ from the reference program's by a relative error of at most 0.005.
Values may be sent and summed in bfloat16 or wider, within the bound.
A program may use at most 128 MiB of HBM per device.

```python
import jax
import jax.numpy as jnp
from jax import lax

D = 6144
FF = 24576
TOKENS = 512
FF_COL = 6144
N_COL = 4


def levels(stream_key, shape, split, smallest, largest):
    def one(position, blocks):
        steps = jax.random.uniform(jax.random.fold_in(jax.random.fold_in(stream_key, 6), position), (blocks,), jnp.float32, smallest / len(split), largest / len(split))
        return jnp.repeat(jnp.exp(steps), shape[position] // blocks).reshape((-1,) + (1,) * (len(shape) - position - 1))

    loudness = one(*split[0])
    for cut in split[1:]:
        loudness = loudness * one(*cut)
    return loudness


def scatter_about(own_key, shape, spread, bound, cuts=(), held_as=jnp.bfloat16):
    level = levels(own_key, shape, cuts, -0.22, 0.18) if cuts else 1.0
    array = jax.random.normal(own_key, shape, jnp.float32) * spread * level
    return jnp.minimum(jnp.maximum(array, -bound), bound).astype(held_as)


def setup_inputs(seed: int = 0) -> dict:
    keys = jax.random.split(jax.random.key(seed), 4)
    inputs = scatter_about(keys[0], (TOKENS, D), 1.0, 6.0, ((0, 2), (1, 4)))
    weight = scatter_about(keys[1], (D, FF), D ** -0.5, 0.078125, ((0, 4), (1, 4)))
    cotangent = scatter_about(keys[2], (TOKENS, N_COL, FF_COL), 1.0, 6.0, ((0, 2), (1, 4), (2, 4)))
    return dict(inputs=inputs, weight=weight, cotangent=cotangent)


root_two_pi = 0.7978845608028654
cubic = 0.044715


def reference(inputs, weight, cotangent):
    hidden = jnp.dot(inputs, weight, preferred_element_type=jnp.float32)
    inner = root_two_pi * (hidden + cubic * hidden * hidden * hidden)
    tanh_val = jnp.tanh(inner)
    activated = (0.5 * hidden * (1.0 + tanh_val)).astype(jnp.bfloat16).reshape(TOKENS, N_COL, FF // N_COL)
    slope = 0.5 * (1.0 + tanh_val) + 0.5 * hidden * (1.0 - tanh_val * tanh_val) * root_two_pi * (1.0 + 3.0 * cubic * hidden * hidden)
    flat_cot = cotangent.reshape(TOKENS, FF)
    grad_hidden = (flat_cot.astype(jnp.float32) * slope).astype(jnp.bfloat16)
    input_grad = lax.dot_general(grad_hidden, weight, (((1,), (1,)), ((), ())), preferred_element_type=jnp.float32).astype(jnp.bfloat16)
    weight_full = lax.dot_general(inputs, grad_hidden, (((0,), (0,)), ((), ())), preferred_element_type=jnp.float32)
    weight_grad = weight_full.astype(jnp.bfloat16).reshape(D, N_COL, FF // N_COL)
    return activated, input_grad, weight_grad
```

```python
import functools

import jax
import jax.numpy as jnp
from jax import lax
from jax.experimental import pallas as pl
from jax.experimental.pallas import tpu as pltpu
from jax.sharding import PartitionSpec as P

root_two_pi = 0.7978845608028654
cubic = 0.044715
MESH = pl.DeviceIdType.MESH


def remote(src, dst, send_sem, recv_sem, where):
    return pltpu.make_async_remote_copy(
        src_ref=src,
        dst_ref=dst,
        send_sem=send_sem,
        recv_sem=recv_sem,
        device_id=where,
        device_id_type=MESH,
    )


def kernel(
    rows, depths, cols, x_ref, w_hbm, cot_hbm,
    act_out, grad_out, x_all, g_all,
    w_buf, part, s_buf, r_buf, l_buf, g_buf, cot_buf, act_buf, acc, out_buf, in_buf,
    w_sem, cot_sem, act_sem, s_sem, r_sem, l_sem, g_sem, gr_sem, gl_sem, xs_sem, xr_sem,
    in_sem, out_sem, cs_sem, cr_sem,
):
    r, d, c = lax.axis_index("row"), lax.axis_index("depth"), lax.axis_index("col")
    tokens, features = x_ref.shape
    chunk = w_buf.shape[2]
    steps = w_buf.shape[0] // rows
    width = steps * chunk
    per = rows // depths
    last = rows - 1
    twin = c + 1 - 2 * lax.rem(c, 2)
    bits = cols.bit_length() - 1

    def flip(bit):
        size = 1 << bit
        return c + size - 2 * size * lax.rem(c // size, 2)

    def w_copy(q, k):
        j = q * steps + k
        at = pl.multiple_of(q * width + k * chunk, chunk)
        return pltpu.make_async_copy(w_hbm.at[:, pl.ds(at, chunk)], w_buf.at[j], w_sem.at[j])

    def cot_copy(k):
        at = pl.multiple_of(k * chunk, chunk)
        return pltpu.make_async_copy(cot_hbm.at[:, pl.ds(at, chunk)], cot_buf.at[k], cot_sem.at[k])

    def act_copy(k):
        at = pl.multiple_of(k * chunk, chunk)
        return pltpu.make_async_copy(act_buf.at[k], act_out.at[:, pl.ds(at, chunk)], act_sem.at[k])

    def right(j):
        return remote(s_buf.at[j], r_buf.at[j], s_sem.at[j], r_sem.at[j], {"row": r + 1})

    def left(j):
        return remote(s_buf.at[j], l_buf.at[j], s_sem.at[j], l_sem.at[j], {"row": r - 1})

    def g_right(j):
        return remote(g_buf.at[j], g_buf.at[j], gr_sem.at[j], g_sem.at[j], {"row": r + 1})

    def g_left(j):
        return remote(g_buf.at[j], g_buf.at[j], gl_sem.at[j], g_sem.at[j], {"row": r - 1})

    def g_place(source, q, k):
        at = pl.multiple_of(lax.rem(q, per) * width + k * chunk, chunk)
        return g_all.at[pl.ds(pl.multiple_of(source * tokens, tokens), tokens), pl.ds(at, chunk)]

    def g_over(q, k):
        j = q * steps + k
        slot = (d * per + lax.rem(q, per)) * steps + k
        return remote(
            g_buf.at[j], g_place(d, q, k), xs_sem.at[j], xr_sem.at[slot], {"depth": q // per}
        )

    def g_keep(q, k):
        j = q * steps + k
        return pltpu.make_async_copy(g_buf.at[j], g_place(d, q, k), xs_sem.at[j])

    def share(q, k):
        @pl.when(q // per != d)
        def _():
            g_over(q, k).start()

        @pl.when(q // per == d)
        def _():
            g_keep(q, k).start()

    def x_place(source):
        return x_all.at[pl.ds(pl.multiple_of(source * tokens, tokens), tokens), :]

    def x_over(target):
        return remote(
            x_ref, x_place(d), in_sem.at[target], out_sem.at[d], {"depth": target}
        )

    x_keep = pltpu.make_async_copy(x_ref, x_place(d), in_sem.at[d])

    for k in range(steps):
        for q in range(rows):
            w_copy(q, k).start()
        cot_copy(k).start()
    x_keep.start()

    barrier = pltpu.get_barrier_semaphore()

    @pl.when(r > 0)
    def _():
        pl.semaphore_signal(barrier, inc=1, device_id={"row": r - 1}, device_id_type=MESH)

    @pl.when(r < last)
    def _():
        pl.semaphore_signal(barrier, inc=1, device_id={"row": r + 1}, device_id_type=MESH)

    for off in range(1, depths):
        pl.semaphore_signal(
            barrier, inc=1, device_id={"depth": lax.rem(d + off, depths)}, device_id_type=MESH
        )
    for bit in range(bits):
        pl.semaphore_signal(barrier, inc=1, device_id={"col": flip(bit)}, device_id_type=MESH)

    @pl.when((r > 0) & (r < last))
    def _():
        pl.semaphore_wait(barrier, depths + bits + 1)

    @pl.when((r == 0) | (r == last))
    def _():
        pl.semaphore_wait(barrier, depths + bits)

    for off in range(1, depths):
        x_over(lax.rem(d + off, depths)).start()

    acc[...] = jnp.zeros_like(acc)

    def body(s, carry):
        @pl.when(s < steps)
        def _():
            for q in range(rows):
                j = q * steps + s
                w_copy(q, s).wait()
                part[j] = jnp.dot(x_ref[...], w_buf[j], preferred_element_type=jnp.float32)

        kr = s - r

        @pl.when((kr >= 0) & (kr < steps))
        def _():
            for q in range(last, 0, -1):
                @pl.when(q > r)
                def _():
                    j = q * steps + kr

                    @pl.when(r > 0)
                    def _():
                        right(j).wait_recv()
                        s_buf[j] = (part[j] + r_buf[j].astype(jnp.float32)).astype(jnp.bfloat16)

                    @pl.when(r == 0)
                    def _():
                        s_buf[j] = part[j].astype(jnp.bfloat16)

                    right(j).start()

        kl = s - (last - r)

        @pl.when((kl >= 0) & (kl < steps))
        def _():
            for q in range(last):
                @pl.when(q < r)
                def _():
                    j = q * steps + kl

                    @pl.when(r < last)
                    def _():
                        left(j).wait_recv()
                        s_buf[j] = (part[j] + l_buf[j].astype(jnp.float32)).astype(jnp.bfloat16)

                    @pl.when(r == last)
                    def _():
                        s_buf[j] = part[j].astype(jnp.bfloat16)

                    left(j).start()

        ke = s - last

        @pl.when((ke >= 0) & (ke < steps))
        def _():
            j = r * steps + ke

            @pl.when(r > 0)
            def _():
                right(j).wait_recv()
                part[j] = part[j] + r_buf[j].astype(jnp.float32)

            @pl.when(r < last)
            def _():
                left(j).wait_recv()
                part[j] = part[j] + l_buf[j].astype(jnp.float32)

            cot_copy(ke).wait()
            hidden = part[j]
            square = hidden * hidden
            tanh_val = jnp.tanh(root_two_pi * (hidden + cubic * square * hidden))
            half = 0.5 * (1.0 + tanh_val)
            act_buf[ke] = (hidden * half).astype(jnp.bfloat16)
            slope = half + 0.5 * hidden * (1.0 - tanh_val * tanh_val) * root_two_pi * (
                1.0 + 3.0 * cubic * square
            )
            g_buf[j] = (cot_buf[ke].astype(jnp.float32) * slope).astype(jnp.bfloat16)

            @pl.when(r < last)
            def _():
                g_right(j).start()

            @pl.when(r > 0)
            def _():
                g_left(j).start()

            act_copy(ke).start()
            share(r, ke)

        for away in range(1, rows):
            kg = s - last - away

            @pl.when((kg >= 0) & (kg < steps) & (r - away >= 0))
            def _():
                q = r - away
                j = q * steps + kg
                g_right(j).wait_recv()

                @pl.when(r < last)
                def _():
                    g_right(j).start()

                share(q, kg)

            @pl.when((kg >= 0) & (kg < steps) & (r + away <= last))
            def _():
                q = r + away
                j = q * steps + kg
                g_left(j).wait_recv()

                @pl.when(r > 0)
                def _():
                    g_left(j).start()

                share(q, kg)

        ki = s - 2 * last

        @pl.when((ki >= 0) & (ki < steps))
        def _():
            wide = 512 if features % 512 == 0 else features
            for n in range(0, features, wide):
                total = acc[:, n : n + wide]
                for q in range(rows):
                    j = q * steps + ki
                    total = total + lax.dot_general(
                        g_buf[j],
                        w_buf[j, n : n + wide, :],
                        (((1,), (1,)), ((), ())),
                        preferred_element_type=jnp.float32,
                    )
                acc[:, n : n + wide] = total

        return carry

    lax.fori_loop(0, steps + 2 * last, body, 0)

    half_rows = tokens // 2
    mine = lax.rem(c, 2)
    own_rows = pl.ds(pl.multiple_of(mine * half_rows, half_rows), half_rows)
    other_rows = pl.ds(pl.multiple_of((1 - mine) * half_rows, half_rows), half_rows)
    out_buf[0] = acc[other_rows, :].astype(jnp.bfloat16)
    swap = remote(out_buf.at[0], in_buf.at[0], cs_sem.at[0], cr_sem.at[0], {"col": twin})
    swap.start()
    swap.wait()
    out_buf[1] = (acc[own_rows, :] + in_buf[0].astype(jnp.float32)).astype(jnp.bfloat16)
    for bit in range(1, bits):
        swap = remote(
            out_buf.at[bit], in_buf.at[bit], cs_sem.at[bit], cr_sem.at[bit], {"col": flip(bit)}
        )
        swap.start()
        swap.wait()
        out_buf[bit + 1] = (
            out_buf[bit].astype(jnp.float32) + in_buf[bit].astype(jnp.float32)
        ).astype(jnp.bfloat16)
    result = out_buf.at[bits]
    final = remote(result, grad_out.at[own_rows, :], cs_sem.at[bits], cr_sem.at[bits], {"col": twin})
    keep = pltpu.make_async_copy(result, grad_out.at[own_rows, :], cs_sem.at[bits + 1])
    final.start()
    keep.start()

    for off in range(1, depths):
        target = lax.rem(d + off, depths)
        x_over(target).wait_send()
        source = lax.rem(d + depths - off, depths)
        remote(x_ref, x_place(source), in_sem.at[target], out_sem.at[source], {"depth": target}).wait_recv()
    x_keep.wait()

    def drain(k, carry):
        act_copy(k).wait()
        for q in range(rows):
            j = q * steps + k

            @pl.when(q > r)
            def _():
                right(j).wait_send()

            @pl.when(q < r)
            def _():
                left(j).wait_send()

            @pl.when((q <= r) & (r < last))
            def _():
                g_right(j).wait_send()

            @pl.when((q >= r) & (r > 0))
            def _():
                g_left(j).wait_send()

            @pl.when(q // per != d)
            def _():
                g_over(q, k).wait_send()

            @pl.when(q // per == d)
            def _():
                g_keep(q, k).wait()

        for off in range(1, depths):
            source = lax.rem(d + off, depths)
            for p in range(per):
                slot = (source * per + p) * steps + k
                remote(
                    g_buf.at[k], g_place(source, p, k), xs_sem.at[k], xr_sem.at[slot], {"depth": source}
                ).wait_recv()
        return carry

    lax.fori_loop(0, steps, drain, 0)
    keep.wait()
    final.wait_send()
    remote(
        result, grad_out.at[other_rows, :], cs_sem.at[bits], cr_sem.at[bits], {"col": twin}
    ).wait_recv()


def local(rows, depths, cols, inputs, weight, cotangent):
    tokens, features = inputs.shape
    units = weight.shape[1]
    width = units // rows
    chunk = 256 if width % 256 == 0 else width
    steps = width // chunk
    blocks = rows * steps
    bits = cols.bit_length() - 1
    bf16, f32 = jnp.bfloat16, jnp.float32
    dma = lambda n: pltpu.SemaphoreType.DMA((n,))
    anywhere = pl.BlockSpec(memory_space=pl.ANY)
    activated, input_grad, x_all, g_all = pl.pallas_call(
        functools.partial(kernel, rows, depths, cols),
        out_shape=(
            jax.ShapeDtypeStruct((tokens, width), bf16),
            jax.ShapeDtypeStruct((tokens, features), bf16),
            jax.ShapeDtypeStruct((depths * tokens, features), bf16),
            jax.ShapeDtypeStruct((depths * tokens, units // depths), bf16),
        ),
        in_specs=[pl.BlockSpec(memory_space=pltpu.VMEM), anywhere, anywhere],
        out_specs=(anywhere,) * 4,
        scratch_shapes=[
            pltpu.VMEM((blocks, features, chunk), bf16),
            pltpu.VMEM((blocks, tokens, chunk), f32),
            pltpu.VMEM((blocks, tokens, chunk), bf16),
            pltpu.VMEM((blocks, tokens, chunk), bf16),
            pltpu.VMEM((blocks, tokens, chunk), bf16),
            pltpu.VMEM((blocks, tokens, chunk), bf16),
            pltpu.VMEM((steps, tokens, chunk), bf16),
            pltpu.VMEM((steps, tokens, chunk), bf16),
            pltpu.VMEM((tokens, features), f32),
            pltpu.VMEM((bits + 1, tokens // 2, features), bf16),
            pltpu.VMEM((bits, tokens // 2, features), bf16),
            dma(blocks), dma(steps), dma(steps), dma(blocks), dma(blocks), dma(blocks),
            dma(blocks), dma(blocks), dma(blocks), dma(blocks), dma(depths * (rows // depths) * steps),
            dma(depths), dma(depths), dma(bits + 2), dma(bits + 1),
        ],
        compiler_params=pltpu.CompilerParams(
            collective_id=0, has_side_effects=True, vmem_limit_bytes=60 * 1024 * 1024
        ),
    )(inputs, weight, cotangent[:, 0, :])
    weight_grad = lax.dot_general(
        x_all, g_all, (((0,), (0,)), ((), ())), preferred_element_type=f32
    ).astype(bf16)
    return activated[:, None, :], input_grad, weight_grad[:, None, :]


def solution(mesh):
    shape = mesh.shape
    placed = (P("depth", "row"), P("row", "col"), P("depth", "col", "row"))
    return jax.shard_map(
        functools.partial(local, shape["row"], shape["depth"], shape["col"]),
        mesh=mesh,
        in_specs=placed,
        out_specs=(P("depth", "col", "row"), P("depth", "row"), P("row", "col", "depth")),
        check_vma=False,
    )
```

```python
import functools

import jax
import jax.numpy as jnp
from jax import lax
from jax.experimental import pallas as pl
from jax.experimental.pallas import tpu as pltpu
from jax.sharding import PartitionSpec as P

root_two_pi = 0.7978845608028654
cubic = 0.044715
MESH = pl.DeviceIdType.MESH


def remote(src, dst, send_sem, recv_sem, where):
    return pltpu.make_async_remote_copy(
        src_ref=src,
        dst_ref=dst,
        send_sem=send_sem,
        recv_sem=recv_sem,
        device_id=where,
        device_id_type=MESH,
    )


def kernel(
    rows, depths, cols, groups, x_ref, w_hbm, cot_hbm,
    act_out, grad_out, x_all, g_all,
    w_buf, part, s_buf, r_buf, l_buf, g_buf, cot_buf, act_buf, acc, out_buf, in_buf,
    w_sem, cot_sem, act_sem, s_sem, r_sem, l_sem, g_sem, gr_sem, gl_sem, xs_sem, xr_sem,
    in_sem, out_sem, cs_sem, cr_sem,
):
    r, d, c = lax.axis_index("row"), lax.axis_index("depth"), lax.axis_index("col")
    tokens, features = x_ref.shape
    chunk = w_buf.shape[2]
    parts = w_buf.shape[0] // rows
    steps = parts * groups
    width = parts * chunk
    span = tokens // groups
    per = rows // depths
    last = rows - 1
    twin = c + 1 - 2 * lax.rem(c, 2)
    bits = cols.bit_length() - 1

    def flip(bit):
        size = 1 << bit
        return c + size - 2 * size * lax.rem(c // size, 2)

    def w_copy(q, k):
        j = q * parts + k
        at = pl.multiple_of(q * width + k * chunk, chunk)
        return pltpu.make_async_copy(w_hbm.at[:, pl.ds(at, chunk)], w_buf.at[j], w_sem.at[j])

    def rows_of(k, base):
        return pl.ds(pl.multiple_of(base + lax.div(k, parts) * span, span), span)

    def cols_of(k, base):
        return pl.ds(pl.multiple_of(base + lax.rem(k, parts) * chunk, chunk), chunk)

    def cot_copy(k):
        return pltpu.make_async_copy(
            cot_hbm.at[rows_of(k, 0), cols_of(k, 0)], cot_buf.at[k], cot_sem.at[k]
        )

    def act_copy(k):
        return pltpu.make_async_copy(
            act_buf.at[k], act_out.at[rows_of(k, 0), cols_of(k, 0)], act_sem.at[k]
        )

    def right(j):
        return remote(s_buf.at[j], r_buf.at[j], s_sem.at[j], r_sem.at[j], {"row": r + 1})

    def left(j):
        return remote(s_buf.at[j], l_buf.at[j], s_sem.at[j], l_sem.at[j], {"row": r - 1})

    def g_right(j):
        return remote(g_buf.at[j], g_buf.at[j], gr_sem.at[j], g_sem.at[j], {"row": r + 1})

    def g_left(j):
        return remote(g_buf.at[j], g_buf.at[j], gl_sem.at[j], g_sem.at[j], {"row": r - 1})

    def g_place(source, q, k):
        return g_all.at[rows_of(k, source * tokens), cols_of(k, lax.rem(q, per) * width)]

    def g_over(q, k):
        j = q * steps + k
        slot = (d * per + lax.rem(q, per)) * steps + k
        return remote(
            g_buf.at[j], g_place(d, q, k), xs_sem.at[j], xr_sem.at[slot], {"depth": q // per}
        )

    def g_keep(q, k):
        j = q * steps + k
        return pltpu.make_async_copy(g_buf.at[j], g_place(d, q, k), xs_sem.at[j])

    def share(q, k):
        @pl.when(q // per != d)
        def _():
            g_over(q, k).start()

        @pl.when(q // per == d)
        def _():
            g_keep(q, k).start()

    def x_place(source):
        return x_all.at[pl.ds(pl.multiple_of(source * tokens, tokens), tokens), :]

    def x_over(target):
        return remote(
            x_ref, x_place(d), in_sem.at[target], out_sem.at[d], {"depth": target}
        )

    x_keep = pltpu.make_async_copy(x_ref, x_place(d), in_sem.at[d])

    for k in range(parts):
        for q in range(rows):
            w_copy(q, k).start()

    def fetch(k, carry):
        cot_copy(k).start()
        return carry

    lax.fori_loop(0, steps, fetch, 0)
    x_keep.start()

    barrier = pltpu.get_barrier_semaphore()

    @pl.when(r > 0)
    def _():
        pl.semaphore_signal(barrier, inc=1, device_id={"row": r - 1}, device_id_type=MESH)

    @pl.when(r < last)
    def _():
        pl.semaphore_signal(barrier, inc=1, device_id={"row": r + 1}, device_id_type=MESH)

    for off in range(1, depths):
        pl.semaphore_signal(
            barrier, inc=1, device_id={"depth": lax.rem(d + off, depths)}, device_id_type=MESH
        )
    for bit in range(bits):
        pl.semaphore_signal(barrier, inc=1, device_id={"col": flip(bit)}, device_id_type=MESH)

    @pl.when((r > 0) & (r < last))
    def _():
        pl.semaphore_wait(barrier, depths + bits + 1)

    @pl.when((r == 0) | (r == last))
    def _():
        pl.semaphore_wait(barrier, depths + bits)

    for off in range(1, depths):
        x_over(lax.rem(d + off, depths)).start()

    acc[...] = jnp.zeros_like(acc)

    def project(k):
        if isinstance(k, int):
            k = jnp.int32(k)
        p = lax.rem(k, parts)

        @pl.when(k < parts)
        def _():
            for q in range(rows):
                w_copy(q, p).wait()

        for q in range(rows):
            part[q * steps + k] = jnp.dot(
                x_ref[rows_of(k, 0), :], w_buf[q * parts + p], preferred_element_type=jnp.float32
            )

    def lag(q):
        return jnp.maximum(q, last - q)

    half = span // 2
    mine = lax.rem(c, 2)

    def half_at(t, which):
        return pl.ds(pl.multiple_of(t * span + which * half, half), half)

    def swap(t, bit):
        return remote(
            out_buf.at[bit, t], in_buf.at[bit, t], cs_sem.at[bit, t], cr_sem.at[bit, t],
            {"col": flip(bit)},
        )

    def final(t, which):
        return remote(
            out_buf.at[bits, t], grad_out.at[half_at(t, which), :], cs_sem.at[bits, t],
            cr_sem.at[bits, t], {"col": twin},
        )

    def keep(t):
        return pltpu.make_async_copy(
            out_buf.at[bits, t], grad_out.at[half_at(t, mine), :], cs_sem.at[bits + 1, t]
        )

    def ended(k):
        return (k >= 0) & (k < steps) & (lax.rem(k, parts) == parts - 1)

    project(0)

    def body(s, carry):
        kr = s - r

        @pl.when((kr >= 0) & (kr < steps))
        def _():
            for q in range(last, 0, -1):
                @pl.when(q > r)
                def _():
                    j = q * steps + kr

                    @pl.when(r > 0)
                    def _():
                        right(j).wait_recv()
                        s_buf[j] = (part[j] + r_buf[j].astype(jnp.float32)).astype(jnp.bfloat16)

                    @pl.when(r == 0)
                    def _():
                        s_buf[j] = part[j].astype(jnp.bfloat16)

                    right(j).start()

        kl = s - (last - r)

        @pl.when((kl >= 0) & (kl < steps))
        def _():
            for q in range(last):
                @pl.when(q < r)
                def _():
                    j = q * steps + kl

                    @pl.when(r < last)
                    def _():
                        left(j).wait_recv()
                        s_buf[j] = (part[j] + l_buf[j].astype(jnp.float32)).astype(jnp.bfloat16)

                    @pl.when(r == last)
                    def _():
                        s_buf[j] = part[j].astype(jnp.bfloat16)

                    left(j).start()

        ke = s - lag(r)

        @pl.when((ke >= 0) & (ke < steps))
        def _():
            j = r * steps + ke

            @pl.when(r > 0)
            def _():
                right(j).wait_recv()
                part[j] = part[j] + r_buf[j].astype(jnp.float32)

            @pl.when(r < last)
            def _():
                left(j).wait_recv()
                part[j] = part[j] + l_buf[j].astype(jnp.float32)

            cot_copy(ke).wait()
            hidden = part[j]
            square = hidden * hidden
            tanh_val = jnp.tanh(root_two_pi * (hidden + cubic * square * hidden))
            gate = 0.5 * (1.0 + tanh_val)
            act_buf[ke] = (hidden * gate).astype(jnp.bfloat16)
            slope = gate + 0.5 * hidden * (1.0 - tanh_val * tanh_val) * root_two_pi * (
                1.0 + 3.0 * cubic * square
            )
            g_buf[j] = (cot_buf[ke].astype(jnp.float32) * slope).astype(jnp.bfloat16)

            @pl.when(r < last)
            def _():
                g_right(j).start()

            @pl.when(r > 0)
            def _():
                g_left(j).start()

            act_copy(ke).start()
            share(r, ke)

        for away in range(1, rows):
            ka = s - lag(r - away) - away

            @pl.when((ka >= 0) & (ka < steps) & (r - away >= 0))
            def _():
                q = r - away
                j = q * steps + ka
                g_right(j).wait_recv()

                @pl.when(r < last)
                def _():
                    g_right(j).start()

                share(q, ka)

            kb = s - lag(r + away) - away

            @pl.when((kb >= 0) & (kb < steps) & (r + away <= last))
            def _():
                q = r + away
                j = q * steps + kb
                g_left(j).wait_recv()

                @pl.when(r > 0)
                def _():
                    g_left(j).start()

                share(q, kb)

        @pl.when(s + 1 < steps)
        def _():
            project(s + 1)

        ki = s - 2 * last

        @pl.when((ki >= 0) & (ki < steps))
        def _():
            p = lax.rem(ki, parts)
            wide = 512 if features % 512 == 0 else features
            for n in range(0, features, wide):
                total = acc[rows_of(ki, 0), n : n + wide]
                for q in range(rows):
                    total = total + lax.dot_general(
                        g_buf[q * steps + ki],
                        w_buf[q * parts + p, n : n + wide, :],
                        (((1,), (1,)), ((), ())),
                        preferred_element_type=jnp.float32,
                    )
                acc[rows_of(ki, 0), n : n + wide] = total

        @pl.when(ended(ki))
        def _():
            t = lax.div(ki, parts)
            out_buf[0, t] = acc[half_at(t, 1 - mine), :].astype(jnp.bfloat16)
            swap(t, 0).start()

        for bit in range(bits):
            kc = ki - 1 - 2 * bit

            @pl.when(ended(kc))
            def _():
                t = lax.div(kc, parts)
                swap(t, bit).wait_recv()
                own = acc[half_at(t, mine), :] if bit == 0 else out_buf[bit, t].astype(jnp.float32)
                out_buf[bit + 1, t] = (own + in_buf[bit, t].astype(jnp.float32)).astype(jnp.bfloat16)
                if bit + 1 < bits:
                    swap(t, bit + 1).start()
                else:
                    final(t, mine).start()
                    keep(t).start()

        return carry

    lax.fori_loop(0, steps + 2 * last + 2 * bits - 1, body, 0)

    for off in range(1, depths):
        target = lax.rem(d + off, depths)
        x_over(target).wait_send()
        source = lax.rem(d + depths - off, depths)
        remote(x_ref, x_place(source), in_sem.at[target], out_sem.at[source], {"depth": target}).wait_recv()
    x_keep.wait()

    def drain(k, carry):
        act_copy(k).wait()
        for q in range(rows):
            j = q * steps + k

            @pl.when(q > r)
            def _():
                right(j).wait_send()

            @pl.when(q < r)
            def _():
                left(j).wait_send()

            @pl.when((q <= r) & (r < last))
            def _():
                g_right(j).wait_send()

            @pl.when((q >= r) & (r > 0))
            def _():
                g_left(j).wait_send()

            @pl.when(q // per != d)
            def _():
                g_over(q, k).wait_send()

            @pl.when(q // per == d)
            def _():
                g_keep(q, k).wait()

        for off in range(1, depths):
            source = lax.rem(d + off, depths)
            for p in range(per):
                slot = (source * per + p) * steps + k
                remote(
                    g_buf.at[k], g_place(source, p, k), xs_sem.at[k], xr_sem.at[slot], {"depth": source}
                ).wait_recv()
        return carry

    lax.fori_loop(0, steps, drain, 0)
    for t in range(groups):
        for bit in range(bits):
            swap(t, bit).wait_send()
        keep(t).wait()
        final(t, mine).wait_send()
        final(t, 1 - mine).wait_recv()


def local(rows, depths, cols, inputs, weight, cotangent):
    tokens, features = inputs.shape
    units = weight.shape[1]
    width = units // rows
    groups = 2
    chunk = 256 if width % 256 == 0 else width
    parts = width // chunk
    steps = parts * groups
    span = tokens // groups
    blocks = rows * steps
    bits = cols.bit_length() - 1
    bf16, f32 = jnp.bfloat16, jnp.float32
    dma = lambda *n: pltpu.SemaphoreType.DMA(n)
    anywhere = pl.BlockSpec(memory_space=pl.ANY)
    activated, input_grad, x_all, g_all = pl.pallas_call(
        functools.partial(kernel, rows, depths, cols, groups),
        out_shape=(
            jax.ShapeDtypeStruct((tokens, width), bf16),
            jax.ShapeDtypeStruct((tokens, features), bf16),
            jax.ShapeDtypeStruct((depths * tokens, features), bf16),
            jax.ShapeDtypeStruct((depths * tokens, units // depths), bf16),
        ),
        in_specs=[pl.BlockSpec(memory_space=pltpu.VMEM), anywhere, anywhere],
        out_specs=(anywhere,) * 4,
        scratch_shapes=[
            pltpu.VMEM((rows * parts, features, chunk), bf16),
            pltpu.VMEM((blocks, span, chunk), f32),
            pltpu.VMEM((blocks, span, chunk), bf16),
            pltpu.VMEM((blocks, span, chunk), bf16),
            pltpu.VMEM((blocks, span, chunk), bf16),
            pltpu.VMEM((blocks, span, chunk), bf16),
            pltpu.VMEM((steps, span, chunk), bf16),
            pltpu.VMEM((steps, span, chunk), bf16),
            pltpu.VMEM((tokens, features), f32),
            pltpu.VMEM((bits + 1, groups, span // 2, features), bf16),
            pltpu.VMEM((bits, groups, span // 2, features), bf16),
            dma(rows * parts), dma(steps), dma(steps), dma(blocks), dma(blocks), dma(blocks),
            dma(blocks), dma(blocks), dma(blocks), dma(blocks), dma(depths * (rows // depths) * steps),
            dma(depths), dma(depths), dma(bits + 2, groups), dma(bits + 1, groups),
        ],
        compiler_params=pltpu.CompilerParams(
            collective_id=0, has_side_effects=True, vmem_limit_bytes=60 * 1024 * 1024
        ),
    )(inputs, weight, cotangent[:, 0, :])
    weight_grad = lax.dot_general(
        x_all, g_all, (((0,), (0,)), ((), ())), preferred_element_type=f32
    ).astype(bf16)
    return activated[:, None, :], input_grad, weight_grad[:, None, :]


def solution(mesh):
    shape = mesh.shape
    placed = (P("depth", "row"), P("row", "col"), P("depth", "col", "row"))
    return jax.shard_map(
        functools.partial(local, shape["row"], shape["depth"], shape["col"]),
        mesh=mesh,
        in_specs=placed,
        out_specs=(P("depth", "col", "row"), P("depth", "row"), P("row", "col", "depth")),
        check_vma=False,
    )
```

```python
import functools

import jax
import jax.numpy as jnp
from jax import lax
from jax.experimental import pallas as pl
from jax.experimental.pallas import tpu as pltpu
from jax.sharding import PartitionSpec as P

root_two_pi = 0.7978845608028654
cubic = 0.044715
MESH = pl.DeviceIdType.MESH


def remote(src, dst, send_sem, recv_sem, where):
    return pltpu.make_async_remote_copy(
        src_ref=src,
        dst_ref=dst,
        send_sem=send_sem,
        recv_sem=recv_sem,
        device_id=where,
        device_id_type=MESH,
    )


def kernel(
    rows, depths, cols, groups, x_ref, w_hbm, cot_hbm,
    act_out, grad_out, x_all, g_all,
    w_buf, part, s_buf, r_buf, l_buf, g_buf, cot_buf, act_buf, acc, out_buf, in_buf,
    w_sem, cot_sem, act_sem, s_sem, r_sem, l_sem, g_sem, gr_sem, gl_sem, xs_sem, xr_sem,
    in_sem, out_sem, cs_sem, cr_sem,
):
    r, d, c = lax.axis_index("row"), lax.axis_index("depth"), lax.axis_index("col")
    tokens, features = x_ref.shape
    chunk = w_buf.shape[2]
    parts = w_buf.shape[0] // rows
    steps = parts * groups
    width = parts * chunk
    span = tokens // groups
    per = rows // depths
    last = rows - 1
    twin = c + 1 - 2 * lax.rem(c, 2)
    bits = cols.bit_length() - 1

    def flip(bit):
        size = 1 << bit
        return c + size - 2 * size * lax.rem(c // size, 2)

    def w_copy(q, k):
        j = q * parts + k
        at = pl.multiple_of(q * width + k * chunk, chunk)
        return pltpu.make_async_copy(w_hbm.at[:, pl.ds(at, chunk)], w_buf.at[j], w_sem.at[j])

    def rows_of(k, base):
        return pl.ds(pl.multiple_of(base + lax.div(k, parts) * span, span), span)

    def cols_of(k, base):
        return pl.ds(pl.multiple_of(base + lax.rem(k, parts) * chunk, chunk), chunk)

    def cot_copy(k):
        return pltpu.make_async_copy(
            cot_hbm.at[rows_of(k, 0), cols_of(k, 0)], cot_buf.at[k], cot_sem.at[k]
        )

    def act_copy(k):
        return pltpu.make_async_copy(
            act_buf.at[k], act_out.at[rows_of(k, 0), cols_of(k, 0)], act_sem.at[k]
        )

    def right(j):
        return remote(s_buf.at[j], r_buf.at[j], s_sem.at[j], r_sem.at[j], {"row": r + 1})

    def left(j):
        return remote(s_buf.at[j], l_buf.at[j], s_sem.at[j], l_sem.at[j], {"row": r - 1})

    def g_right(j):
        return remote(g_buf.at[j], g_buf.at[j], gr_sem.at[j], g_sem.at[j], {"row": r + 1})

    def g_left(j):
        return remote(g_buf.at[j], g_buf.at[j], gl_sem.at[j], g_sem.at[j], {"row": r - 1})

    def g_place(source, q, k):
        return g_all.at[rows_of(k, source * tokens), cols_of(k, lax.rem(q, per) * width)]

    def g_over(q, k):
        j = q * steps + k
        slot = (d * per + lax.rem(q, per)) * steps + k
        return remote(
            g_buf.at[j], g_place(d, q, k), xs_sem.at[j], xr_sem.at[slot], {"depth": q // per}
        )

    def g_keep(q, k):
        j = q * steps + k
        return pltpu.make_async_copy(g_buf.at[j], g_place(d, q, k), xs_sem.at[j])

    def share(q, k):
        @pl.when(q // per != d)
        def _():
            g_over(q, k).start()

        @pl.when(q // per == d)
        def _():
            g_keep(q, k).start()

    def x_place(source):
        return x_all.at[pl.ds(pl.multiple_of(source * tokens, tokens), tokens), :]

    def x_over(target):
        return remote(
            x_ref, x_place(d), in_sem.at[target], out_sem.at[d], {"depth": target}
        )

    x_keep = pltpu.make_async_copy(x_ref, x_place(d), in_sem.at[d])

    for k in range(min(2, parts)):
        for q in range(rows):
            w_copy(q, k).start()

    def fetch(k, carry):
        cot_copy(k).start()
        return carry

    lax.fori_loop(0, steps, fetch, 0)
    x_keep.start()

    barrier = pltpu.get_barrier_semaphore()

    @pl.when(r > 0)
    def _():
        pl.semaphore_signal(barrier, inc=1, device_id={"row": r - 1}, device_id_type=MESH)

    @pl.when(r < last)
    def _():
        pl.semaphore_signal(barrier, inc=1, device_id={"row": r + 1}, device_id_type=MESH)

    for off in range(1, depths):
        pl.semaphore_signal(
            barrier, inc=1, device_id={"depth": lax.rem(d + off, depths)}, device_id_type=MESH
        )
    for bit in range(bits):
        pl.semaphore_signal(barrier, inc=1, device_id={"col": flip(bit)}, device_id_type=MESH)

    @pl.when((r > 0) & (r < last))
    def _():
        pl.semaphore_wait(barrier, depths + bits + 1)

    @pl.when((r == 0) | (r == last))
    def _():
        pl.semaphore_wait(barrier, depths + bits)

    for off in range(1, depths):
        x_over(lax.rem(d + off, depths)).start()

    acc[...] = jnp.zeros_like(acc)

    def project(k):
        if isinstance(k, int):
            k = jnp.int32(k)
        p = lax.rem(k, parts)

        @pl.when(k < parts)
        def _():
            for q in range(rows):
                w_copy(q, p).wait()

        @pl.when(k + 2 < parts)
        def _():
            for q in range(rows):
                w_copy(q, p + 2).start()

        for q in range(rows):
            part[q * steps + k] = jnp.dot(
                x_ref[rows_of(k, 0), :], w_buf[q * parts + p], preferred_element_type=jnp.float32
            )

    def lag(q):
        return jnp.maximum(q, last - q)

    half = span // 2
    mine = lax.rem(c, 2)

    def half_at(t, which):
        return pl.ds(pl.multiple_of(t * span + which * half, half), half)

    def swap(t, bit):
        return remote(
            out_buf.at[bit, t], in_buf.at[bit, t], cs_sem.at[bit, t], cr_sem.at[bit, t],
            {"col": flip(bit)},
        )

    def final(t, which):
        return remote(
            out_buf.at[bits, t], grad_out.at[half_at(t, which), :], cs_sem.at[bits, t],
            cr_sem.at[bits, t], {"col": twin},
        )

    def keep(t):
        return pltpu.make_async_copy(
            out_buf.at[bits, t], grad_out.at[half_at(t, mine), :], cs_sem.at[bits + 1, t]
        )

    def ended(k):
        return (k >= 0) & (k < steps) & (lax.rem(k, parts) == parts - 1)

    project(0)

    def body(s, carry):
        kr = s - r

        @pl.when((kr >= 0) & (kr < steps))
        def _():
            for q in range(last, 0, -1):
                @pl.when(q > r)
                def _():
                    j = q * steps + kr

                    @pl.when(r > 0)
                    def _():
                        right(j).wait_recv()
                        s_buf[j] = (part[j] + r_buf[j].astype(jnp.float32)).astype(jnp.bfloat16)

                    @pl.when(r == 0)
                    def _():
                        s_buf[j] = part[j].astype(jnp.bfloat16)

                    right(j).start()

        kl = s - (last - r)

        @pl.when((kl >= 0) & (kl < steps))
        def _():
            for q in range(last):
                @pl.when(q < r)
                def _():
                    j = q * steps + kl

                    @pl.when(r < last)
                    def _():
                        left(j).wait_recv()
                        s_buf[j] = (part[j] + l_buf[j].astype(jnp.float32)).astype(jnp.bfloat16)

                    @pl.when(r == last)
                    def _():
                        s_buf[j] = part[j].astype(jnp.bfloat16)

                    left(j).start()

        ke = s - lag(r)

        @pl.when((ke >= 0) & (ke < steps))
        def _():
            j = r * steps + ke

            @pl.when(r > 0)
            def _():
                right(j).wait_recv()
                part[j] = part[j] + r_buf[j].astype(jnp.float32)

            @pl.when(r < last)
            def _():
                left(j).wait_recv()
                part[j] = part[j] + l_buf[j].astype(jnp.float32)

            cot_copy(ke).wait()
            hidden = part[j]
            square = hidden * hidden
            tanh_val = jnp.tanh(root_two_pi * (hidden + cubic * square * hidden))
            gate = 0.5 * (1.0 + tanh_val)
            act_buf[ke] = (hidden * gate).astype(jnp.bfloat16)
            slope = gate + 0.5 * hidden * (1.0 - tanh_val * tanh_val) * root_two_pi * (
                1.0 + 3.0 * cubic * square
            )
            g_buf[j] = (cot_buf[ke].astype(jnp.float32) * slope).astype(jnp.bfloat16)

            @pl.when(r < last)
            def _():
                g_right(j).start()

            @pl.when(r > 0)
            def _():
                g_left(j).start()

            act_copy(ke).start()
            share(r, ke)

        for away in range(1, rows):
            ka = s - lag(r - away) - away

            @pl.when((ka >= 0) & (ka < steps) & (r - away >= 0))
            def _():
                q = r - away
                j = q * steps + ka
                g_right(j).wait_recv()

                @pl.when(r < last)
                def _():
                    g_right(j).start()

                share(q, ka)

            kb = s - lag(r + away) - away

            @pl.when((kb >= 0) & (kb < steps) & (r + away <= last))
            def _():
                q = r + away
                j = q * steps + kb
                g_left(j).wait_recv()

                @pl.when(r > 0)
                def _():
                    g_left(j).start()

                share(q, kb)

        @pl.when(s + 1 < steps)
        def _():
            project(s + 1)

        ki = s - 2 * last

        @pl.when((ki >= 0) & (ki < steps))
        def _():
            p = lax.rem(ki, parts)
            wide = 512 if features % 512 == 0 else features
            for n in range(0, features, wide):
                total = acc[rows_of(ki, 0), n : n + wide]
                for q in range(rows):
                    total = total + lax.dot_general(
                        g_buf[q * steps + ki],
                        w_buf[q * parts + p, n : n + wide, :],
                        (((1,), (1,)), ((), ())),
                        preferred_element_type=jnp.float32,
                    )
                acc[rows_of(ki, 0), n : n + wide] = total

        @pl.when(ended(ki))
        def _():
            t = lax.div(ki, parts)
            out_buf[0, t] = acc[half_at(t, 1 - mine), :].astype(jnp.bfloat16)
            swap(t, 0).start()

        for bit in range(bits):
            kc = ki - 1 - 2 * bit

            @pl.when(ended(kc))
            def _():
                t = lax.div(kc, parts)
                swap(t, bit).wait_recv()
                own = acc[half_at(t, mine), :] if bit == 0 else out_buf[bit, t].astype(jnp.float32)
                out_buf[bit + 1, t] = (own + in_buf[bit, t].astype(jnp.float32)).astype(jnp.bfloat16)
                if bit + 1 < bits:
                    swap(t, bit + 1).start()
                else:
                    final(t, mine).start()
                    keep(t).start()

        return carry

    lax.fori_loop(0, steps + 2 * last + 2 * bits - 1, body, 0)

    for off in range(1, depths):
        target = lax.rem(d + off, depths)
        x_over(target).wait_send()
        source = lax.rem(d + depths - off, depths)
        remote(x_ref, x_place(source), in_sem.at[target], out_sem.at[source], {"depth": target}).wait_recv()
    x_keep.wait()

    def drain(k, carry):
        act_copy(k).wait()
        for q in range(rows):
            j = q * steps + k

            @pl.when(q > r)
            def _():
                right(j).wait_send()

            @pl.when(q < r)
            def _():
                left(j).wait_send()

            @pl.when((q <= r) & (r < last))
            def _():
                g_right(j).wait_send()

            @pl.when((q >= r) & (r > 0))
            def _():
                g_left(j).wait_send()

            @pl.when(q // per != d)
            def _():
                g_over(q, k).wait_send()

            @pl.when(q // per == d)
            def _():
                g_keep(q, k).wait()

        for off in range(1, depths):
            source = lax.rem(d + off, depths)
            for p in range(per):
                slot = (source * per + p) * steps + k
                remote(
                    g_buf.at[k], g_place(source, p, k), xs_sem.at[k], xr_sem.at[slot], {"depth": source}
                ).wait_recv()
        return carry

    lax.fori_loop(0, steps, drain, 0)
    for t in range(groups):
        for bit in range(bits):
            swap(t, bit).wait_send()
        keep(t).wait()
        final(t, mine).wait_send()
        final(t, 1 - mine).wait_recv()


def local(rows, depths, cols, inputs, weight, cotangent):
    tokens, features = inputs.shape
    units = weight.shape[1]
    width = units // rows
    groups = 2
    chunk = 256 if width % 256 == 0 else width
    parts = width // chunk
    steps = parts * groups
    span = tokens // groups
    blocks = rows * steps
    bits = cols.bit_length() - 1
    bf16, f32 = jnp.bfloat16, jnp.float32
    dma = lambda *n: pltpu.SemaphoreType.DMA(n)
    anywhere = pl.BlockSpec(memory_space=pl.ANY)
    activated, input_grad, x_all, g_all = pl.pallas_call(
        functools.partial(kernel, rows, depths, cols, groups),
        out_shape=(
            jax.ShapeDtypeStruct((tokens, width), bf16),
            jax.ShapeDtypeStruct((tokens, features), bf16),
            jax.ShapeDtypeStruct((depths * tokens, features), bf16),
            jax.ShapeDtypeStruct((depths * tokens, units // depths), bf16),
        ),
        in_specs=[pl.BlockSpec(memory_space=pltpu.VMEM), anywhere, anywhere],
        out_specs=(anywhere,) * 4,
        scratch_shapes=[
            pltpu.VMEM((rows * parts, features, chunk), bf16),
            pltpu.VMEM((blocks, span, chunk), f32),
            pltpu.VMEM((blocks, span, chunk), bf16),
            pltpu.VMEM((blocks, span, chunk), bf16),
            pltpu.VMEM((blocks, span, chunk), bf16),
            pltpu.VMEM((blocks, span, chunk), bf16),
            pltpu.VMEM((steps, span, chunk), bf16),
            pltpu.VMEM((steps, span, chunk), bf16),
            pltpu.VMEM((tokens, features), f32),
            pltpu.VMEM((bits + 1, groups, span // 2, features), bf16),
            pltpu.VMEM((bits, groups, span // 2, features), bf16),
            dma(rows * parts), dma(steps), dma(steps), dma(blocks), dma(blocks), dma(blocks),
            dma(blocks), dma(blocks), dma(blocks), dma(blocks), dma(depths * (rows // depths) * steps),
            dma(depths), dma(depths), dma(bits + 2, groups), dma(bits + 1, groups),
        ],
        compiler_params=pltpu.CompilerParams(
            collective_id=0, has_side_effects=True, vmem_limit_bytes=60 * 1024 * 1024
        ),
    )(inputs, weight, cotangent[:, 0, :])
    weight_grad = lax.dot_general(
        x_all, g_all, (((0,), (0,)), ((), ())), preferred_element_type=f32
    ).astype(bf16)
    return activated[:, None, :], input_grad, weight_grad[:, None, :]


def solution(mesh):
    shape = mesh.shape
    placed = (P("depth", "row"), P("row", "col"), P("depth", "col", "row"))
    return jax.shard_map(
        functools.partial(local, shape["row"], shape["depth"], shape["col"]),
        mesh=mesh,
        in_specs=placed,
        out_specs=(P("depth", "col", "row"), P("depth", "row"), P("row", "col", "depth")),
        check_vma=False,
    )
```
